768 devices in a mesh: dp: 384 (over z, y, x), fsdp: 2 (over core).
Axes of the slice: x: 4, y: 8, z: 12, core: 2. Of those that a mesh axis runs over, the one named last changes fastest.
Arguments:
- patches: bfloat16 [196608, 1280], P(('dp', 'fsdp')), may hold values from -6 to 6
- queries: bfloat16 [196608, 1280], P(('dp', 'fsdp')), may hold values from -200 to 200
- key_in: bfloat16 [196608, 1280], P(('dp', 'fsdp')), may hold values from -200 to 200
- values: bfloat16 [196608, 1280], P(('dp', 'fsdp')), may hold values from -6 to 6
- windows: int32 [768, 256], P(('dp', 'fsdp')), may hold values from 0 to 7, never falling along the last dimension, each value on 1 to 64 neighbouring positions
- out_weight: bfloat16 [1280, 1280], P('fsdp'), may hold values from -0.15625 to 0.15625
- owners: int32 [196608, 1], P(('dp', 'fsdp')), may hold values from 0 to 1; in each aligned block of 256 rows (0 to 255, 256 to 511, ...) at most 256 rows name the same one
- grad_out: bfloat16 [196608, 1280], P(('dp', 'fsdp')), may hold values from -6 to 6
Outputs:
- returned: bfloat16 [393216, 1280], P(('dp', 'fsdp'))
- grad_wo: float32 [1280, 1280], P('fsdp')
The draws below stay inside these ranges and needn't reach their ends.
Inputs may be any that keep to these rules, and one draw needn't show every extreme that they name: `windows`: window ids never fall along a device's rows; each window holds 1 to 64 rows, some window exactly 64. `owners`: among the rows of one device at most 256 name the same owner, and in every draw some device's owner takes exactly 256.
All inputs are finite; a program needn't handle non-finite values.
Results may differ from the reference program's by a relative error of at most 0.007.
Values may be sent and summed in bfloat16 or wider, within the bound.
A program may use at most 64 MiB of HBM per device.

```python
import math
import jax
import jax.numpy as jnp
import numpy as np
from jax import lax

D = 1280
HEADS = 16
HEAD_DIM = 80
WINDOW = 64
P_DEV = 256
CAP = 256
ROWS = 196608
N_DP = 384
N_FSDP = 2


def draw_queries(key, part):
    key = jax.random.fold_in(key, 11)
    return jax.random.normal(key, (ROWS, D), jnp.float32).astype(jnp.bfloat16)


def draw_key_in(key, part):
    key = jax.random.fold_in(key, 23)
    return jax.random.normal(key, (ROWS, D), jnp.float32).astype(jnp.bfloat16)


def steps_of(own_key, extent, shards, smallest, high):
    factor_of, own = 1.0, jax.random.fold_in(own_key, 6)
    for position, blocks in shards:
        steps = jnp.exp(jax.random.uniform(jax.random.fold_in(own, position), (blocks,), jnp.float32, smallest / len(shards), high / len(shards)))
        factor_of = factor_of * jnp.repeat(steps, extent[position] // blocks).reshape([-1 if axis == position else 1 for axis in range(len(extent))])
    return factor_of


def length_profile(count, total, reach, skew):
    weights = [(1 << 20) // math.isqrt(standing ** skew) + 1 for standing in range(2, count + 1)]
    spare, given = total - reach - (count - 1), [1] * (count - 1)
    while spare > 0:
        free = [i for i in range(count - 1) if given[i] < reach]
        whole, budget = sum([weights[i] for i in free]), spare
        for i in free:
            addition = min(reach - given[i], max(1, budget * weights[i] // whole), spare)
            given[i] = given[i] + addition
            spare = spare - addition
    return np.array([reach] + given)


def ragged_sizes(key, count, total, bound, skew):
    if count == 2:
        one = jax.random.randint(key, (), max(1, total - bound), min(bound, total - 1) + 1)
        return jnp.stack([one, total - one])
    lengths = jnp.asarray(length_profile(count, total, bound, skew), jnp.int32)
    twos = (count - 1) // 2
    donor, taker = lengths[1:1 + 2 * twos:2], lengths[2:2 + 2 * twos:2]
    room = jnp.minimum(donor - 1, bound - taker)
    moved = jax.random.randint(jax.random.fold_in(key, 1), (twos,), 0, 1 << 20) % (room + 1)
    lengths = lengths.at[1:1 + 2 * twos:2].set(donor - moved).at[2:2 + 2 * twos:2].set(taker + moved)
    return lengths[jax.random.permutation(jax.random.fold_in(key, 2), count)]


def assign_block(key, own, number, rows, count, top, limit, lean):
    order = jax.random.permutation(key, count)
    crowded, usual = load_shares(count, rows * top, limit, lean, True), load_shares(count, rows * top, limit, lean, False)
    places = jnp.arange(count)

    def named(sizes, turn):
        used = int((sizes > 0).sum())
        fixed = max(1, used // 4)
        shifted = fixed + (places - fixed + turn * (used - fixed)) % max(1, count - fixed)
        return jnp.zeros((count,), jnp.int32).at[order[jnp.where(places < fixed, places, shifted)]].set(jnp.asarray(sizes, jnp.int32))

    sizes = jnp.where(number % 4 == 0, named(crowded, number // 4), named(usual, number - number // 4 - 1))
    mixed = jax.random.permutation(jax.random.fold_in(own, 3), count)
    donor, receiver = mixed[0:count // 2 * 2:2], mixed[1:count // 2 * 2:2]
    slack = jnp.minimum(sizes[donor] - 1, limit - sizes[receiver]) // 2
    slack = jnp.where((donor == order[0]) | (receiver == order[0]) | (sizes[receiver] == 0), 0, jnp.maximum(slack, 0))
    shifted = jax.random.randint(jax.random.fold_in(own, 4), (count // 2,), 0, 1 << 20) % (slack + 1)
    sizes = sizes.at[donor].add(-shifted).at[receiver].add(shifted)
    items = jnp.searchsorted(jnp.cumsum(sizes), jnp.arange(rows * top), side="right").astype(jnp.int32)
    listing = items.reshape(top, rows).T
    listing = listing[jax.random.permutation(jax.random.fold_in(own, 1), rows)]
    turn = jax.random.randint(jax.random.fold_in(own, 2), (rows, 1), 0, top)
    return jnp.take_along_axis(listing, (jnp.arange(top)[None, :] + turn) % top, axis=1)


def load_shares(count, total, reach, slope, full):
    weights = [(1 << 20) // math.isqrt(rank ** slope) + 1 for rank in range(1, count + 1)]
    largest = reach if full else min(reach, max(-(-total // count), total * weights[0] // sum(weights)))
    least = 1 if total - largest >= count - 1 else 0
    counts, surplus = [largest] + [least] * (count - 1), total - largest - least * (count - 1)
    while surplus > 0:
        movable = [i for i in range(1, count) if counts[i] < largest] or [i for i in range(1, count) if counts[i] < reach]
        mass, left = sum([weights[i] for i in movable]), surplus
        for i in movable:
            addition = min(reach - counts[i], max(1, left * weights[i] // mass), surplus)
            counts[i] = counts[i] + addition
            surplus = surplus - addition
    return np.array(counts)


def centred(stream_key, shape, deviation, most, shards=(), held_as=jnp.bfloat16):
    values = jax.random.normal(stream_key, shape, jnp.float32) * deviation
    if len(shards) > 0:
        values = steps_of(stream_key, shape, shards, -0.22, 0.18) * values
    return jnp.clip(values, min=-most, max=most).astype(held_as)


def setup_inputs(seed: int = 0) -> dict:
    keys = jax.random.split(jax.random.key(seed), 9)
    patches = centred(keys[0], (ROWS, D), 1.0, 6.0, ((0, 768),))
    queries = draw_queries(jax.random.fold_in(keys[8], 71), 0)
    key_in = draw_key_in(jax.random.fold_in(keys[8], 71), 0)
    values = centred(keys[3], (ROWS, D), 1.0, 6.0, ((0, 768),))
    windows = jax.vmap(lambda own: jnp.searchsorted(jnp.cumsum(ragged_sizes(own, 2 * P_DEV // WINDOW, P_DEV, WINDOW, 1)), jnp.arange(P_DEV), side="right"))(jax.random.split(keys[4], (N_DP * N_FSDP))).reshape((N_DP * N_FSDP, P_DEV)).astype(jnp.int32)
    out_weight = centred(keys[5], (D, D), D ** -0.5, 0.15625, ((0, 2),))
    owners_keys = jax.random.split(jax.random.fold_in(keys[6], 1), ROWS // P_DEV)
    owners_turns = jax.random.permutation(jax.random.fold_in(keys[6], 3), ROWS // P_DEV)
    owners = jax.vmap(lambda own, number: assign_block(jax.random.fold_in(keys[6], 2), own, number, P_DEV, N_FSDP, 1, CAP, 2))(owners_keys, owners_turns).reshape((ROWS, 1))
    grad_out = centred(keys[7], (ROWS, D), 1.0, 6.0, ((0, 768),))
    return {"patches": patches, "queries": queries, "key_in": key_in, "values": values, "windows": windows, "out_weight": out_weight, "owners": owners, "grad_out": grad_out}


def attend(queries, key_in, values, window_ids):
    length = queries.shape[0]
    query_heads = queries.reshape(length, HEADS, HEAD_DIM).astype(jnp.float32)
    key_heads = key_in.reshape(length, HEADS, HEAD_DIM).astype(jnp.float32)
    value_heads = values.reshape(length, HEADS, HEAD_DIM).astype(jnp.float32)
    scores = jnp.einsum('qhd,khd->hqk', query_heads, key_heads) / math.sqrt(HEAD_DIM)
    same_window = window_ids[:, None] == window_ids[None, :]
    scores = jnp.where(same_window[None], scores, -1e+30)
    highest = lax.optimization_barrier(jnp.max(scores, axis=-1, keepdims=True))
    expo = jnp.exp(scores - highest)
    weights = (expo / lax.optimization_barrier(jnp.sum(expo, axis=-1, keepdims=True))).astype(jnp.bfloat16)
    attended = jnp.einsum('hqk,khd->qhd', weights.astype(jnp.float32), value_heads)
    return attended.reshape(length, HEADS * HEAD_DIM).astype(jnp.bfloat16)

def place_rows(encoded, owner_ids, groups, capacity):
    onehot = (owner_ids[:, None] == jnp.arange(groups, dtype=jnp.int32)[None, :]).astype(jnp.int32)
    ranking = lax.optimization_barrier(jnp.sum((jnp.cumsum(onehot, axis=0) - 1) * onehot, axis=1)).astype(jnp.int32)
    positions = (owner_ids.astype(jnp.int32) * capacity + ranking).astype(jnp.int32)
    empty = jnp.zeros((groups * capacity, encoded.shape[1]), jnp.bfloat16)
    return empty.at[positions].set(encoded)

def reference(patches, queries, key_in, values, windows, out_weight, owners, grad_out):
    devices = N_DP * N_FSDP
    capacity = 2 * P_DEV // N_FSDP

    def per_device(array):
        return array.reshape(devices, P_DEV, array.shape[1])

    def visit(running, packed):
        patch_rows, query_rows, key_rows, value_rows, window_ids, owner_ids, cotangent = packed
        attended = attend(query_rows, key_rows, value_rows, window_ids)
        projected = jnp.dot(attended, out_weight, preferred_element_type=jnp.float32)
        encoded = (patch_rows.astype(jnp.float32) + projected).astype(jnp.bfloat16)
        buffer = place_rows(encoded, owner_ids, N_FSDP, capacity)
        partial_value = lax.dot_general(attended, cotangent, (((0,), (0,)), ((), ())), preferred_element_type=jnp.float32)
        partial_value = lax.optimization_barrier(partial_value.astype(jnp.bfloat16)).astype(jnp.float32)
        return (running + partial_value, buffer)
    summed, buffers = lax.scan(visit, jnp.zeros((D, D), jnp.float32), (per_device(patches), per_device(queries), per_device(key_in), per_device(values), windows, owners.reshape(devices, P_DEV), per_device(grad_out)))
    returned = buffers.reshape(N_DP, N_FSDP, N_FSDP, capacity, D).transpose(0, 2, 1, 3, 4)
    returned = returned.reshape(devices * N_FSDP * capacity, D)
    grad_wo = summed * (1.0 / math.sqrt(ROWS))
    return (returned, grad_wo)
```

```python
import math

import jax
import jax.numpy as jnp
from jax import lax
from jax.sharding import Mesh
from jax.sharding import PartitionSpec as P

HEADS = 16
HEAD_DIM = 80


def attend(queries, key_in, values, window_ids):
    length = queries.shape[0]
    query_heads = queries.reshape(length, HEADS, HEAD_DIM)
    key_heads = key_in.reshape(length, HEADS, HEAD_DIM)
    value_heads = values.reshape(length, HEADS, HEAD_DIM)
    scores = jnp.einsum(
        "qhd,khd->hqk", query_heads, key_heads, preferred_element_type=jnp.float32
    ) / math.sqrt(HEAD_DIM)
    same_window = window_ids[:, None] == window_ids[None, :]
    scores = jnp.where(same_window[None], scores, -1e30)
    highest = jnp.max(scores, axis=-1, keepdims=True)
    expo = jnp.exp(scores - highest)
    weights = (expo / jnp.sum(expo, axis=-1, keepdims=True)).astype(jnp.bfloat16)
    attended = jnp.einsum("hqk,khd->qhd", weights, value_heads, preferred_element_type=jnp.float32)
    return attended.reshape(length, HEADS * HEAD_DIM).astype(jnp.bfloat16)


def place_rows(encoded, owner_ids, groups, capacity):
    onehot = (owner_ids[:, None] == jnp.arange(groups, dtype=jnp.int32)[None, :]).astype(jnp.int32)
    ranking = jnp.sum((jnp.cumsum(onehot, axis=0) - 1) * onehot, axis=1)
    positions = owner_ids * capacity + ranking
    empty = jnp.zeros((groups * capacity, encoded.shape[1]), jnp.bfloat16)
    return empty.at[positions].set(encoded)


def per_device(patches, queries, key_in, values, windows, out_weight, owners, grad_out):
    length = patches.shape[0]
    groups = lax.axis_size("fsdp")
    replicas = lax.axis_size("x") * lax.axis_size("y") * lax.axis_size("z")
    capacity = 2 * length // groups
    attended = attend(queries, key_in, values, windows[0])
    columns = attended
    projected = jnp.dot(
        columns,
        lax.all_gather(out_weight, "fsdp", axis=0, tiled=True),
        preferred_element_type=jnp.float32,
    )
    encoded = (patches.astype(jnp.float32) + projected).astype(jnp.bfloat16)
    buffer = place_rows(encoded, owners[:, 0], groups, capacity)
    returned = lax.all_to_all(buffer, "fsdp", split_axis=0, concat_axis=0, tiled=True)
    columns = attended
    partial_value = lax.dot_general(
        columns, grad_out, (((0,), (0,)), ((), ())), preferred_element_type=jnp.float32
    )
    shard_sum = lax.psum_scatter(
        lax.optimization_barrier(partial_value.astype(jnp.bfloat16))
        .astype(jnp.float32)
        .astype(jnp.bfloat16),
        "fsdp",
        scatter_dimension=0,
        tiled=True,
    ).astype(jnp.float32)
    piece = lax.psum_scatter(shard_sum, "x", scatter_dimension=0, tiled=True)
    piece = lax.psum_scatter(piece, "y", scatter_dimension=1, tiled=True)
    piece = lax.psum(piece, "z")
    piece = lax.all_gather(piece, "y", axis=1, tiled=True)
    summed = lax.all_gather(piece, "x", axis=0, tiled=True)
    factor = 1.0 / math.sqrt(length * groups * replicas)
    grad_wo = summed * factor
    return (returned, grad_wo)


def solution(mesh):
    grid = Mesh(mesh.devices.reshape(12, 8, 4, 2), ("z", "y", "x", "fsdp"))
    rows = P(("z", "y", "x", "fsdp"), None)
    return jax.shard_map(
        per_device,
        mesh=grid,
        in_specs=(rows, rows, rows, rows, rows, P("fsdp", None), rows, rows),
        out_specs=(rows, P("fsdp", None)),
        check_vma=False,
    )
```

```python
import functools
import math

import jax
import jax.numpy as jnp
from jax import lax
from jax.experimental import pallas as pl
from jax.experimental.pallas import tpu as pltpu
from jax.sharding import Mesh
from jax.sharding import PartitionSpec as P

HEADS = 16
HEAD_DIM = 80
MESH = pl.DeviceIdType.MESH
ROW, LANE = 16, 128
PARTS = ((7, ("x", "y", "z")), (3, ("y", "x", "z")))


def attend(queries, key_in, values, window_ids):
    length = queries.shape[0]
    query_heads = queries.reshape(length, HEADS, HEAD_DIM)
    key_heads = key_in.reshape(length, HEADS, HEAD_DIM)
    value_heads = values.reshape(length, HEADS, HEAD_DIM)
    scores = jnp.einsum(
        "qhd,khd->hqk", query_heads, key_heads, preferred_element_type=jnp.float32
    ) / math.sqrt(HEAD_DIM)
    same_window = window_ids[:, None] == window_ids[None, :]
    scores = jnp.where(same_window[None], scores, -1e30)
    highest = jnp.max(scores, axis=-1, keepdims=True)
    expo = jnp.exp(scores - highest)
    weights = (expo / jnp.sum(expo, axis=-1, keepdims=True)).astype(jnp.bfloat16)
    attended = jnp.einsum("hqk,khd->qhd", weights, value_heads, preferred_element_type=jnp.float32)
    return attended.reshape(length, HEADS * HEAD_DIM).astype(jnp.bfloat16)


class Part:
    def __init__(self, first, blocks, order, sizes, rows):
        self.first, self.blocks, self.order = first, blocks, order
        self.per_block = rows // ROW
        self.tiles = blocks * self.per_block
        n = [sizes[axis] for axis in order]
        self.n = n
        t1 = -(-self.tiles // n[0])
        t2 = -(-t1 // n[1])
        t3 = -(-t2 // n[2])
        t2 = -(-t2 // t3) * t3
        t1 = -(-t1 // t2) * t2
        self.take = (t1, t2, t3)
        self.owners = (-(-self.tiles // t1), t1 // t2, t2 // t3)
        self.padded = self.owners[0] * t1

    def scratch(self):
        held = {"sum0": pltpu.VMEM((self.padded, ROW, LANE), jnp.bfloat16)}
        for k in range(3):
            n, take = self.n[k], self.take[k]
            held[f"in{k}"] = pltpu.VMEM((n - 1, take, ROW, LANE), jnp.bfloat16)
            if k < 2:
                held[f"sum{k + 1}"] = pltpu.VMEM((take, ROW, LANE), jnp.bfloat16)
            for name in ("rs_send", "rs_recv", "ag_send", "ag_recv"):
                held[f"{name}{k}"] = pltpu.SemaphoreType.DMA((n - 1,))
        held["all"] = pltpu.VMEM((self.padded, ROW, LANE), jnp.bfloat16)
        return held


def among(condition, always, step):
    if always:
        step()
    else:
        pl.when(condition)(step)


def reduce_copies(part, held, k):
    axis, n, take, owners = part.order[k], part.n[k], part.take[k], part.owners[k]
    me = lax.axis_index(axis)
    for d in range(1, n):
        peer = lax.rem(me + d, n)
        run = peer if owners == n else jnp.minimum(peer, owners - 1)
        yield pltpu.make_async_remote_copy(
            src_ref=held[f"sum{k}"].at[pl.ds(run * take, take)],
            dst_ref=held[f"in{k}"].at[d - 1],
            send_sem=held[f"rs_send{k}"].at[d - 1],
            recv_sem=held[f"rs_recv{k}"].at[d - 1],
            device_id={axis: peer},
            device_id_type=MESH,
        ), peer < owners, me < owners


def reduce_start(part, held, k):
    always = part.owners[k] == part.n[k]
    for copy, sent, _ in reduce_copies(part, held, k):
        among(sent, always, copy.start)


def reduce_finish(part, held, k, base):
    n, take, owners = part.n[k], part.take[k], part.owners[k]
    me = lax.axis_index(part.order[k])

    def receive():
        for copy, _, _ in reduce_copies(part, held, k):
            copy.wait_recv()
        total = held[f"sum{k}"][pl.ds(me * take, take)].astype(jnp.float32)
        for d in range(1, n):
            total += held[f"in{k}"][d - 1].astype(jnp.float32)
        total = total.astype(jnp.bfloat16)
        if k < 2:
            held[f"sum{k + 1}"][...] = total
        else:
            held["all"][pl.ds(base, take)] = total

    among(me < owners, owners == n, receive)


def gather_copy(part, held, k, bases, d, run):
    axis, n, take, owners = part.order[k], part.n[k], part.take[k], part.owners[k]
    start = bases[k] + (run if owners == n else jnp.minimum(run, owners - 1)) * take
    return pltpu.make_async_remote_copy(
        src_ref=held["all"].at[pl.ds(start, take)],
        dst_ref=held["all"].at[pl.ds(start, take)],
        send_sem=held[f"ag_send{k}"].at[d - 1],
        recv_sem=held[f"ag_recv{k}"].at[d - 1],
        device_id={axis: lax.rem(lax.axis_index(axis) + d, n)},
        device_id_type=MESH,
    )


def gather_sent(part, held, k, bases):
    me, n = lax.axis_index(part.order[k]), part.n[k]
    for d in range(1, n):
        yield gather_copy(part, held, k, bases, d, me), me < part.owners[k]


def gather_received(part, held, k, bases):
    me, n = lax.axis_index(part.order[k]), part.n[k]
    for d in range(1, n):
        source = lax.rem(me + n - d, n)
        yield gather_copy(part, held, k, bases, d, source), source < part.owners[k]


def gather_start(part, held, k, bases):
    always = part.owners[k] == part.n[k]
    for copy, sent in gather_sent(part, held, k, bases):
        among(sent, always, copy.start)


def gather_finish(part, held, k, bases):
    always = part.owners[k] == part.n[k]
    for copy, received in gather_received(part, held, k, bases):
        among(received, always, copy.wait_recv)


def drain(part, held, bases):
    for k in range(3):
        always = part.owners[k] == part.n[k]
        for copy, sent, _ in reduce_copies(part, held, k):
            among(sent, always, copy.wait_send)
        for copy, sent in gather_sent(part, held, k, bases):
            among(sent, always, copy.wait_send)


def exchange(
    parts, sizes, factor,
    attended, grad_out, weight, patches, owner_ids,
    returned, gradient,
    near, scratch,
):
    core = lax.axis_index("fsdp")
    other = 1 - core
    half = weight.shape[0]
    length = attended.shape[0]
    mine = pl.ds(pl.multiple_of(core * half, LANE), half)
    theirs = pl.ds(pl.multiple_of(other * half, LANE), half)
    sems = near["sems"]

    barrier = pltpu.get_barrier_semaphore()
    greeted = 0
    for axis, n in sizes.items():
        me = lax.axis_index(axis)
        for d in range(1, n):
            pl.semaphore_signal(
                barrier, inc=1, device_id={axis: lax.rem(me + d, n)}, device_id_type=MESH
            )
            greeted += 1

    def local(source, target, number):
        copy = pltpu.make_async_copy(source, target, sems.at[number])
        copy.start()
        return copy

    weight_here = local(weight, near["weight"].at[0], 0)
    patches_here = local(patches, near["patches"], 1)

    pl.semaphore_wait(barrier, greeted)

    def across(source, target, number):
        copy = pltpu.make_async_remote_copy(
            src_ref=source,
            dst_ref=target,
            send_sem=sems.at[number],
            recv_sem=sems.at[number + 1],
            device_id={"fsdp": other},
            device_id_type=MESH,
        )
        copy.start()
        return copy

    attended_there = across(attended.at[:, theirs], near["attended"], 2)
    grad_out_there = across(grad_out, near["grad_out"], 4)
    weight_there = across(weight, near["weight"].at[1], 6)

    attended_there.wait_recv()
    grad_out_there.wait_recv()
    rows_in = (((0,), (0,)), ((), ()))
    for part, held in zip(parts, scratch):
        columns = pl.ds(part.first * LANE, part.blocks * LANE)
        product = lax.dot_general(
            attended[:, mine], grad_out[:, columns], rows_in, preferred_element_type=jnp.float32
        ) + lax.dot_general(
            near["attended"][...], near["grad_out"][:, columns], rows_in,
            preferred_element_type=jnp.float32,
        )
        product = product.astype(jnp.bfloat16)
        for block in range(part.blocks):
            held["sum0"][pl.ds(block * part.per_block, part.per_block)] = product[
                :, block * LANE:(block + 1) * LANE
            ].reshape(part.per_block, ROW, LANE)
        spare = part.padded - part.tiles
        if spare:
            held["sum0"][pl.ds(part.tiles, spare)] = jnp.zeros((spare, ROW, LANE), jnp.bfloat16)
        reduce_start(part, held, 0)

    weight_here.wait()
    patches_here.wait()
    weight_there.wait_recv()
    projected = jnp.dot(
        attended[:, mine], near["weight"][0], preferred_element_type=jnp.float32
    ) + jnp.dot(attended[:, theirs], near["weight"][1], preferred_element_type=jnp.float32)
    encoded = (near["patches"][...].astype(jnp.float32) + projected).astype(jnp.bfloat16)
    owner = owner_ids[...]
    earlier = (
        lax.broadcasted_iota(jnp.int32, (length, length), 0)
        < lax.broadcasted_iota(jnp.int32, (length, length), 1)
    ).astype(jnp.bfloat16)
    is_one = jnp.broadcast_to(owner, (ROW, length)).astype(jnp.float32).astype(jnp.bfloat16)
    ones_before = jnp.dot(is_one, earlier, preferred_element_type=jnp.float32)[:1]
    ones_before = ones_before.astype(jnp.int32)
    place = lax.broadcasted_iota(jnp.int32, (1, length), 1)
    rank = jnp.where(owner == 1, ones_before, place - ones_before)
    slot = lax.broadcasted_iota(jnp.int32, (length, length), 0)

    def placed(group):
        chosen = jnp.where(owner == group, rank, -1)
        onehot = (slot == chosen).astype(jnp.float32).astype(jnp.bfloat16)
        return jnp.dot(onehot, encoded, preferred_element_type=jnp.float32).astype(jnp.bfloat16)

    own_rows = pl.ds(pl.multiple_of(core * length, LANE), length)
    other_rows = pl.ds(pl.multiple_of(other * length, LANE), length)
    near["leaving"][...] = placed(other)
    rows_there = across(near["leaving"], near["returned"].at[own_rows], 8)
    near["returned"][own_rows] = placed(core)

    bases = []
    for part in parts:
        i1, i2, i3 = (lax.axis_index(axis) for axis in part.order)
        (t1, t2, t3), (_, m2, m3) = part.take, part.owners
        bases.append((0, i1 * t1, i1 * t1 + i2 * t2, i1 * t1 + i2 * t2 + i3 * t3))

    for k in range(3):
        for part, held, base in zip(parts, scratch, bases):
            reduce_finish(part, held, k, base[3])
            if k < 2:
                reduce_start(part, held, k + 1)
            else:
                gather_start(part, held, 2, base)
        if k == 0:
            rows_there.wait_recv()
            rows_out = local(near["returned"], returned, 10)
    for k in (2, 1, 0):
        for part, held, base in zip(parts, scratch, bases):
            gather_finish(part, held, k, base)
            if k > 0:
                gather_start(part, held, k - 1, base)
            else:
                for block in range(part.blocks):
                    tiles = held["all"][pl.ds(block * part.per_block, part.per_block)]
                    gradient[:, pl.ds((part.first + block) * LANE, LANE)] = (
                        tiles.reshape(half, LANE).astype(jnp.float32) * factor
                    )
    for part, held, base in zip(parts, scratch, bases):
        drain(part, held, base)
    for copy in (attended_there, grad_out_there, weight_there, rows_there):
        copy.wait_send()
    rows_out.wait()


def per_device(patches, queries, key_in, values, windows, out_weight, owners, grad_out):
    sizes = {axis: lax.axis_size(axis) for axis in ("fsdp", "x", "y", "z")}
    length, width = patches.shape
    half = out_weight.shape[0]
    attended = attend(queries, key_in, values, windows[0])
    parts, first = [], 0
    for blocks, order in PARTS:
        parts.append(Part(first, blocks, order, sizes, half))
        first += blocks
    factor = 1.0 / math.sqrt(length * math.prod(sizes.values()))
    bf16 = jnp.bfloat16
    near = {
        "weight": pltpu.VMEM((2, half, width), bf16),
        "patches": pltpu.VMEM((length, width), bf16),
        "attended": pltpu.VMEM((length, half), bf16),
        "grad_out": pltpu.VMEM((length, width), bf16),
        "leaving": pltpu.VMEM((length, width), bf16),
        "returned": pltpu.VMEM((2 * length, width), bf16),
        "sems": pltpu.SemaphoreType.DMA((11,)),
    }
    vmem, anywhere = (pl.BlockSpec(memory_space=space) for space in (pltpu.VMEM, pl.ANY))
    return pl.pallas_call(
        functools.partial(exchange, parts, sizes, factor),
        out_shape=(
            jax.ShapeDtypeStruct((2 * length, width), bf16),
            jax.ShapeDtypeStruct((half, width), jnp.float32),
        ),
        in_specs=[vmem, vmem, anywhere, anywhere, vmem],
        out_specs=(anywhere, vmem),
        scratch_shapes=[near, [part.scratch() for part in parts]],
        compiler_params=pltpu.CompilerParams(
            collective_id=0, has_side_effects=True, vmem_limit_bytes=48 * 1024 * 1024
        ),
    )(attended, grad_out, out_weight, patches, owners.reshape(1, length))


def solution(mesh):
    chips = mesh.devices.reshape(12, 8, 4, 2)
    grid = Mesh(chips, ("z", "y", "x", "fsdp"))
    rows = P(("z", "y", "x", "fsdp"), None)
    return jax.shard_map(
        per_device,
        mesh=grid,
        in_specs=(rows, rows, rows, rows, rows, P("fsdp", None), rows, rows),
        out_specs=(rows, P("fsdp", None)),
        check_vma=False,
    )
```

```python
import functools
import math

import jax
import jax.numpy as jnp
from jax import lax
from jax.experimental import pallas as pl
from jax.experimental.pallas import tpu as pltpu
from jax.sharding import Mesh
from jax.sharding import PartitionSpec as P

HEADS = 16
HEAD_DIM = 80
MESH = pl.DeviceIdType.MESH
ROW, LANE = 16, 128
PARTS = ((4, ("x", "y", "z")), (2, ("y", "x", "z")), (4, ("x", "y", "z")))


def attend_heads(queries, key_in, values, hidden, attended, base):
    width = attended.shape[1]
    pending = {}
    for head in range(width // HEAD_DIM):
        begin = head * HEAD_DIM
        first, last = begin // LANE, (begin + HEAD_DIM - 1) // LANE
        span = (last - first + 1) * LANE
        columns = pl.ds(pl.multiple_of(base + first * LANE, LANE), span)
        place = lax.broadcasted_iota(jnp.int32, (1, span), 1) + (first * LANE - begin)
        own = ((place >= 0) & (place < HEAD_DIM)).astype(jnp.float32).astype(jnp.bfloat16)
        scores = lax.dot_general(
            queries[:, columns] * own, key_in[:, columns], (((1,), (1,)), ((), ())),
            preferred_element_type=jnp.float32,
        ) * (1.0 / math.sqrt(HEAD_DIM)) + hidden[...]
        expo = jnp.exp(scores - jnp.max(scores, axis=1, keepdims=True))
        weights = (expo * (1.0 / jnp.sum(expo, axis=1, keepdims=True))).astype(jnp.bfloat16)
        result = jnp.dot(weights, values[:, columns] * own, preferred_element_type=jnp.float32)
        for block in range(first, last + 1):
            piece = result[:, (block - first) * LANE:(block - first + 1) * LANE]
            pending[block] = pending[block] + piece if block in pending else piece
            if (block + 1) * LANE <= begin + HEAD_DIM:
                attended[:, block * LANE:(block + 1) * LANE] = pending.pop(block).astype(jnp.bfloat16)


class Part:
    def __init__(self, first, blocks, order, sizes, rows):
        self.first, self.blocks, self.order = first, blocks, order
        self.per_block = rows // ROW
        self.tiles = blocks * self.per_block
        n = [sizes[axis] for axis in order]
        self.n = n
        t3 = -(-self.tiles // math.prod(n))
        t2 = -(-self.tiles // (n[0] * n[1]))
        t2 = -(-t2 // t3) * t3
        t1 = n[1] * t2
        self.take = (t1, t2, t3)
        self.owners = (n[0], n[1], t2 // t3)
        self.padded = n[0] * t1
        self.relay = tuple(
            k == 0 and n[k] % 2 == 0 and n[k] >= 4 and self.take[k] >= 2
            for k in range(3)
        )

    def scratch(self):
        held = {"sum0": pltpu.VMEM((self.padded, ROW, LANE), jnp.bfloat16)}
        for k in range(3):
            n, take = self.n[k], self.take[k]
            held[f"in{k}"] = pltpu.VMEM((n - 1, take, ROW, LANE), jnp.bfloat16)
            if k < 2:
                held[f"sum{k + 1}"] = pltpu.VMEM((take, ROW, LANE), jnp.bfloat16)
            for name in ("rs_send", "rs_recv", "ag_send", "ag_recv"):
                held[f"{name}{k}"] = pltpu.SemaphoreType.DMA((n + 2,))
        return held


class Step:
    def __init__(self, part, held, k, bases):
        self.part, self.held, self.k, self.bases = part, held, k, bases
        self.axis, self.n, self.take, self.owners = part.order[k], part.n[k], part.take[k], part.owners[k]
        self.relay, self.everyone = part.relay[k], part.owners[k] == part.n[k]
        self.me = lax.axis_index(self.axis)
        self.far = self.n // 2
        half = self.take // 2
        self.low, self.high = (0, half), (half, self.take - half)
        self.whole = (0, self.take)

    def member(self, d):
        return lax.rem(self.me + d, self.n)

    def run(self, member):
        return (member if self.everyone else jnp.minimum(member, self.owners - 1)) * self.take

    def among(self, member, step):
        if self.everyone:
            step()
        else:
            pl.when(member < self.owners)(step)

    def remote(self, source, target, kind, number, d):
        return pltpu.make_async_remote_copy(
            src_ref=source,
            dst_ref=target,
            send_sem=self.held[f"{kind}_send{self.k}"].at[number],
            recv_sem=self.held[f"{kind}_recv{self.k}"].at[number],
            device_id={self.axis: self.member(d)},
            device_id_type=MESH,
        )

    def given(self):
        if not self.relay:
            return [(d - 1, d, d, self.whole, d - 1) for d in self.nearest_first()], []
        n, far, near = self.n, self.far, self.far - 1
        early = [
            (far - 1, 1, far, self.low, far - 1),
            (n - 1, n - 1, far, self.high, far - 1),
            (near - 1, near, near, self.high, near - 1),
            (n - near - 1, n - near, n - near, self.low, n - near - 1),
        ]
        early += [(d - 1, d, d, self.whole, d - 1) for d in range(1, n) if d not in (near, far, n - near)]
        late = [
            (n, near, near, self.low, near - 1),
            (n + 1, n - near, n - near, self.high, n - near - 1),
        ]
        return early, late

    def nearest_first(self):
        return sorted(range(1, self.n), key=lambda d: -min(d, self.n - d))

    def give(self, copy):
        number, d, owner, (first, count), slot = copy
        start = self.run(self.member(owner)) + first
        return self.remote(
            self.held[f"sum{self.k}"].at[pl.ds(start, count)],
            self.held[f"in{self.k}"].at[slot, pl.ds(first, count)],
            "rs", number, d,
        )

    def reduce_start(self):
        for copy in self.given()[0]:
            self.among(self.member(copy[2]), lambda: self.give(copy).start())

    def reduce_relay(self):
        early, late = self.given()
        for passed, copy in zip(early, late):
            self.give(passed).wait_recv()
            _, _, owner, (first, count), _ = copy
            tiles = pl.ds(self.run(self.member(owner)) + first, count)
            came = self.held[f"in{self.k}"][self.far - 1, pl.ds(first, count)]
            held = self.held[f"sum{self.k}"]
            held[tiles] = (held[tiles].astype(jnp.float32) + came.astype(jnp.float32)).astype(jnp.bfloat16)
            self.give(copy).start()

    def reduce_finish(self):
        k, early, late = self.k, *self.given()

        def receive():
            for copy in early[len(late):] + late:
                self.give(copy).wait_recv()
            total = self.held[f"sum{k}"][pl.ds(self.run(self.me), self.take)].astype(jnp.float32)
            for d in range(1, self.n):
                if not (self.relay and d == self.far):
                    total += self.held[f"in{k}"][d - 1].astype(jnp.float32)
            total = total.astype(jnp.bfloat16)
            if k < 2:
                self.held[f"sum{k + 1}"][...] = total
            else:
                self.held["all"][pl.ds(self.bases[3], self.take)] = total

        self.among(self.me, receive)

    def shown(self):
        if not self.relay:
            return [(d - 1, d, 0, self.whole) for d in self.nearest_first()], []
        n, far, near = self.n, self.far, self.far - 1
        early = [
            (near - 1, near, 0, self.low),
            (n - near - 1, n - near, 0, self.high),
            (n, near, 0, self.high),
            (n + 1, n - near, 0, self.low),
        ]
        early += [(d - 1, d, 0, self.whole) for d in range(1, n) if d not in (near, far, n - near)]
        late = [(far - 1, 1, near, self.low), (n - 1, n - 1, n - near, self.high)]
        return early, late

    def show(self, copy, arriving=False):
        number, d, back, (first, count) = copy
        source = self.member(2 * self.n - back - (d if arriving else 0))
        tiles = pl.ds(self.bases[self.k] + self.run(source) + first, count)
        return self.remote(self.held["all"].at[tiles], self.held["all"].at[tiles], "ag", number, d), source

    def gather_start(self):
        for copy in self.shown()[0]:
            self.among(self.me, lambda: self.show(copy)[0].start())

    def gather_relay(self):
        early, late = self.shown()
        for passed, copy in zip(early, late):
            self.show(passed, True)[0].wait_recv()
            self.show(copy)[0].start()

    def gather_finish(self):
        early, late = self.shown()
        for copy in early[len(late):] + late:
            source = self.member(2 * self.n - copy[2] - copy[1])
            self.among(source, lambda: self.show(copy, True)[0].wait_recv())

    def reduce_drain(self):
        for copy in sum(self.given(), []):
            self.among(self.member(copy[2]), lambda: self.give(copy).wait_send())

    def gather_drain(self):
        for copy in sum(self.shown(), []):
            self.among(self.me, lambda: self.show(copy)[0].wait_send())


def steps_of(parts, scratch):
    steps = [[], [], []]
    for part, held in zip(parts, scratch):
        i1, i2, i3 = (lax.axis_index(axis) for axis in part.order)
        t1, t2, t3 = part.take
        bases = (0, i1 * t1, i1 * t1 + i2 * t2, i1 * t1 + i2 * t2 + i3 * t3)
        for k in range(3):
            steps[k].append(Step(part, held, k, bases))
    return steps


def sum_over_chips(steps, meanwhile):
    for step in steps[0]:
        if step.relay:
            step.reduce_relay()
    write_out = meanwhile()
    for k in range(3):
        for i, step in enumerate(steps[k]):
            step.reduce_finish()
            if k < 2:
                steps[k + 1][i].reduce_start()
            else:
                step.gather_start()
        for step in steps[k]:
            step.reduce_drain()
        if k == 0:
            end = write_out()
    for k in (2, 1, 0):
        for i, step in enumerate(steps[k]):
            if step.relay:
                step.gather_relay()
        for i, step in enumerate(steps[k]):
            step.gather_finish()
            if k > 0:
                steps[k - 1][i].gather_start()
        if k == 1:
            end()
        if k > 0:
            for step in steps[k]:
                step.gather_drain()
    for step in steps[0]:
        step.gather_drain()


def exchange(
    parts, sizes,
    queries, key_in, values, windows_in, owners_in, grad_out, weight, patches,
    returned, *rest,
):
    core = lax.axis_index("fsdp")
    other = 1 - core
    half = weight.shape[0]
    length = queries.shape[0]
    near, scratch = rest[len(parts):]
    scratch = [{**held, "all": total} for held, total in zip(scratch, rest)]
    steps = steps_of(parts, scratch)
    sems = near["sems"]

    barrier = pltpu.get_barrier_semaphore()
    greeted = 0
    for axis, n in sizes.items():
        me = lax.axis_index(axis)
        for d in range(1, n):
            pl.semaphore_signal(
                barrier, inc=1, device_id={axis: lax.rem(me + d, n)}, device_id_type=MESH
            )
            greeted += 1

    def local(source, target, number):
        copy = pltpu.make_async_copy(source, target, sems.at[number])
        copy.start()
        return copy

    windows, owner_ids = near["windows"], near["owners"]
    windows_here = local(windows_in, windows, 12)
    owners_here = local(owners_in, owner_ids, 13)
    grad_out_here = local(grad_out, near["grad_out"].at[0], 0)
    weight_here = local(weight, near["weight"].at[0], 1)
    patches_here = local(patches, near["patches"], 2)

    windows_here.wait()
    ids = jnp.broadcast_to(windows[...].astype(jnp.float32), (length, length))
    near["hidden"][...] = jnp.where(ids == ids.T, 0.0, -1e30)
    arrays = queries, key_in, values, near["hidden"]
    attend_heads(*arrays, near["attended"].at[1], other * half)

    pl.semaphore_wait(barrier, greeted)

    def across(source, target, number):
        copy = pltpu.make_async_remote_copy(
            src_ref=source,
            dst_ref=target,
            send_sem=sems.at[number],
            recv_sem=sems.at[number + 1],
            device_id={"fsdp": other},
            device_id_type=MESH,
        )
        copy.start()
        return copy

    attended_there = across(near["attended"].at[1], near["attended"].at[2], 3)
    grad_out_there = across(grad_out, near["grad_out"].at[1], 5)
    weight_there = across(weight, near["weight"].at[1], 7)
    attend_heads(*arrays, near["attended"].at[0], core * half)

    grad_out_here.wait()
    attended_there.wait_recv()
    grad_out_there.wait_recv()
    rows_in = (((0,), (0,)), ((), ()))
    for part, held, step in zip(parts, scratch, steps[0]):
        columns = pl.ds(part.first * LANE, part.blocks * LANE)
        product = lax.dot_general(
            near["attended"][0], near["grad_out"][0, :, columns], rows_in,
            preferred_element_type=jnp.float32,
        ) + lax.dot_general(
            near["attended"][2], near["grad_out"][1, :, columns], rows_in,
            preferred_element_type=jnp.float32,
        )
        product = product.astype(jnp.bfloat16)
        for block in range(part.blocks):
            held["sum0"][pl.ds(block * part.per_block, part.per_block)] = product[
                :, block * LANE:(block + 1) * LANE
            ].reshape(part.per_block, ROW, LANE)
        spare = part.padded - part.tiles
        if spare:
            held["sum0"][pl.ds(part.tiles, spare)] = jnp.zeros((spare, ROW, LANE), jnp.bfloat16)
        step.reduce_start()

    def encode():
        weight_here.wait()
        patches_here.wait()
        weight_there.wait_recv()
        projected = jnp.dot(
            near["attended"][0], near["weight"][0], preferred_element_type=jnp.float32
        ) + jnp.dot(near["attended"][1], near["weight"][1], preferred_element_type=jnp.float32)
        encoded = (near["patches"][...].astype(jnp.float32) + projected).astype(jnp.bfloat16)
        owners_here.wait()
        owner = owner_ids[...]
        earlier = (
            lax.broadcasted_iota(jnp.int32, (length, length), 0)
            < lax.broadcasted_iota(jnp.int32, (length, length), 1)
        ).astype(jnp.bfloat16)
        is_one = jnp.broadcast_to(owner, (ROW, length)).astype(jnp.float32).astype(jnp.bfloat16)
        ones_before = jnp.dot(is_one, earlier, preferred_element_type=jnp.float32)[:1]
        ones_before = ones_before.astype(jnp.int32)
        place = lax.broadcasted_iota(jnp.int32, (1, length), 1)
        rank = jnp.where(owner == 1, ones_before, place - ones_before)
        slot = lax.broadcasted_iota(jnp.int32, (length, length), 0)

        def placed(group):
            chosen = jnp.where(owner == group, rank, -1)
            onehot = (slot == chosen).astype(jnp.float32).astype(jnp.bfloat16)
            return jnp.dot(onehot, encoded, preferred_element_type=jnp.float32).astype(jnp.bfloat16)

        own_rows = pl.ds(pl.multiple_of(core * length, LANE), length)
        other_rows = pl.ds(pl.multiple_of(other * length, LANE), length)
        near["leaving"][...] = placed(other)
        rows_there = across(near["leaving"], near["returned"].at[own_rows], 9)
        near["returned"][own_rows] = placed(core)

        def write_out():
            rows_there.wait_recv()
            rows_out = local(near["returned"], returned, 11)

            def end():
                rows_there.wait_send()
                rows_out.wait()

            return end

        for copy in (attended_there, grad_out_there, weight_there):
            copy.wait_send()
        return write_out

    sum_over_chips(steps, encode)


def deliver(parts, factor, *refs):
    tiles, (rows, rows_out, gradient, held, sems) = refs[:len(parts)], refs[len(parts):]
    rows_copy = pltpu.make_async_copy(rows, rows_out, sems.at[0])
    rows_copy.start()
    copies = [rows_copy]
    height = held.shape[1]
    deep = height // ROW
    for i in range(held.shape[0]):
        for part, total in zip(parts, tiles):
            for block in range(part.blocks):
                held[i, :, pl.ds((part.first + block) * LANE, LANE)] = (
                    total[pl.ds(block * part.per_block + i * deep, deep)]
                    .reshape(height, LANE).astype(jnp.float32) * factor
                )
        copy = pltpu.make_async_copy(held.at[i], gradient.at[pl.ds(i * height, height)], sems.at[i + 1])
        copy.start()
        copies.append(copy)
    for copy in copies:
        copy.wait()


def per_device(patches, queries, key_in, values, windows, out_weight, owners, grad_out):
    sizes = {axis: lax.axis_size(axis) for axis in ("fsdp", "x", "y", "z")}
    length, width = patches.shape
    half = out_weight.shape[0]
    parts, first = [], 0
    for blocks, order in PARTS:
        parts.append(Part(first, blocks, order, sizes, half))
        first += blocks
    factor = 1.0 / math.sqrt(length * math.prod(sizes.values()))
    bf16 = jnp.bfloat16
    near = {
        "weight": pltpu.VMEM((2, half, width), bf16),
        "patches": pltpu.VMEM((length, width), bf16),
        "windows": pltpu.VMEM((1, length), jnp.int32),
        "owners": pltpu.VMEM((1, length), jnp.int32),
        "hidden": pltpu.VMEM((length, length), jnp.float32),
        "attended": pltpu.VMEM((3, length, half), bf16),
        "grad_out": pltpu.VMEM((2, length, width), bf16),
        "leaving": pltpu.VMEM((length, width), bf16),
        "returned": pltpu.VMEM((2 * length, width), bf16),
        "sems": pltpu.SemaphoreType.DMA((14,)),
    }
    vmem, anywhere, hbm = (
        pl.BlockSpec(memory_space=space) for space in (pltpu.VMEM, pl.ANY, pltpu.HBM)
    )
    params = dict(has_side_effects=True, vmem_limit_bytes=52 * 1024 * 1024)
    returned, *tiles = pl.pallas_call(
        functools.partial(exchange, parts, sizes),
        out_shape=(
            jax.ShapeDtypeStruct((2 * length, width), bf16),
            *(jax.ShapeDtypeStruct((part.padded, ROW, LANE), bf16) for part in parts),
        ),
        in_specs=[vmem] * 3 + [hbm] * 5,
        out_specs=(anywhere, *[vmem] * len(parts)),
        scratch_shapes=[near, [part.scratch() for part in parts]],
        compiler_params=pltpu.CompilerParams(collective_id=0, **params),
        name="exchange",
    )(queries, key_in, values, windows, owners.reshape(1, length), grad_out, out_weight, patches)
    chunks = 4
    return pl.pallas_call(
        functools.partial(deliver, parts, factor),
        out_shape=(
            jax.ShapeDtypeStruct((2 * length, width), bf16),
            jax.ShapeDtypeStruct((half, width), jnp.float32),
        ),
        in_specs=[vmem] * (len(parts) + 1),
        out_specs=(anywhere, anywhere),
        scratch_shapes=[
            pltpu.VMEM((chunks, half // chunks, width), jnp.float32),
            pltpu.SemaphoreType.DMA((chunks + 1,)),
        ],
        compiler_params=pltpu.CompilerParams(**params),
        name="deliver",
    )(*tiles, returned)


def solution(mesh):
    chips = mesh.devices.reshape(12, 8, 4, 2)
    grid = Mesh(chips, ("z", "y", "x", "fsdp"))
    rows = P(("z", "y", "x", "fsdp"), None)
    return jax.shard_map(
        per_device,
        mesh=grid,
        in_specs=(rows, rows, rows, rows, rows, P("fsdp", None), rows, rows),
        out_specs=(rows, P("fsdp", None)),
        check_vma=False,
    )
```

```python
import functools
import math

import jax
import jax.numpy as jnp
from jax import lax
from jax.experimental import pallas as pl
from jax.experimental.pallas import tpu as pltpu
from jax.sharding import Mesh
from jax.sharding import PartitionSpec as P

HEADS = 16
HEAD_DIM = 80
MESH = pl.DeviceIdType.MESH
ROW, LANE = 16, 128
PARTS = ((4, ("x", "y", "z")), (2, ("y", "x", "z")), (4, ("x", "y", "z")))


def attend_heads(queries, key_in, values, hidden, attended, base):
    width = attended.shape[1]
    pending = {}
    for head in range(width // HEAD_DIM):
        begin = head * HEAD_DIM
        first, last = begin // LANE, (begin + HEAD_DIM - 1) // LANE
        span = (last - first + 1) * LANE
        columns = pl.ds(pl.multiple_of(base + first * LANE, LANE), span)
        place = lax.broadcasted_iota(jnp.int32, (1, span), 1) + (first * LANE - begin)
        own = ((place >= 0) & (place < HEAD_DIM)).astype(jnp.float32).astype(jnp.bfloat16)
        scores = lax.dot_general(
            queries[:, columns] * own, key_in[:, columns], (((1,), (1,)), ((), ())),
            preferred_element_type=jnp.float32,
        ) * (1.0 / math.sqrt(HEAD_DIM)) + hidden[...]
        expo = jnp.exp(scores - jnp.max(scores, axis=1, keepdims=True))
        weights = (expo * (1.0 / jnp.sum(expo, axis=1, keepdims=True))).astype(jnp.bfloat16)
        result = jnp.dot(weights, values[:, columns] * own, preferred_element_type=jnp.float32)
        for block in range(first, last + 1):
            piece = result[:, (block - first) * LANE:(block - first + 1) * LANE]
            pending[block] = pending[block] + piece if block in pending else piece
            if (block + 1) * LANE <= begin + HEAD_DIM:
                attended[:, block * LANE:(block + 1) * LANE] = pending.pop(block).astype(jnp.bfloat16)


class Part:
    def __init__(self, first, blocks, order, sizes, rows):
        self.first, self.blocks, self.order = first, blocks, order
        self.per_block = rows // ROW
        self.tiles = blocks * self.per_block
        n = [sizes[axis] for axis in order]
        self.n = n
        t3 = -(-self.tiles // math.prod(n))
        t2 = -(-self.tiles // (n[0] * n[1]))
        t2 = -(-t2 // t3) * t3
        t1 = n[1] * t2
        self.take = (t1, t2, t3)
        self.owners = (n[0], n[1], t2 // t3)
        self.padded = n[0] * t1
        self.relay = tuple(
            k == 0 and n[k] % 2 == 0 and n[k] >= 4 and self.take[k] >= 2
            for k in range(3)
        )

    def scratch(self):
        held = {"sum0": pltpu.VMEM((self.padded, ROW, LANE), jnp.bfloat16)}
        for k in range(3):
            n, take = self.n[k], self.take[k]
            held[f"in{k}"] = pltpu.VMEM((n - 1, take, ROW, LANE), jnp.bfloat16)
            if k < 2:
                held[f"sum{k + 1}"] = pltpu.VMEM((take, ROW, LANE), jnp.bfloat16)
            for name in ("rs_send", "rs_recv", "ag_send", "ag_recv"):
                held[f"{name}{k}"] = pltpu.SemaphoreType.DMA((n + 2,))
        return held


class Step:
    def __init__(self, part, held, k, bases):
        self.part, self.held, self.k, self.bases = part, held, k, bases
        self.axis, self.n, self.take, self.owners = part.order[k], part.n[k], part.take[k], part.owners[k]
        self.relay, self.everyone = part.relay[k], part.owners[k] == part.n[k]
        self.me = lax.axis_index(self.axis)
        self.far = self.n // 2
        half = self.take // 2
        self.low, self.high = (0, half), (half, self.take - half)
        self.whole = (0, self.take)

    def member(self, d):
        return lax.rem(self.me + d, self.n)

    def run(self, member):
        return (member if self.everyone else jnp.minimum(member, self.owners - 1)) * self.take

    def among(self, member, step):
        if self.everyone:
            step()
        else:
            pl.when(member < self.owners)(step)

    def remote(self, source, target, kind, number, d):
        return pltpu.make_async_remote_copy(
            src_ref=source,
            dst_ref=target,
            send_sem=self.held[f"{kind}_send{self.k}"].at[number],
            recv_sem=self.held[f"{kind}_recv{self.k}"].at[number],
            device_id={self.axis: self.member(d)},
            device_id_type=MESH,
        )

    def given(self):
        if not self.relay:
            return [(d - 1, d, d, self.whole, d - 1) for d in self.nearest_first()], []
        n, far, near = self.n, self.far, self.far - 1
        early = [
            (far - 1, 1, far, self.low, far - 1),
            (n - 1, n - 1, far, self.high, far - 1),
            (near - 1, near, near, self.high, near - 1),
            (n - near - 1, n - near, n - near, self.low, n - near - 1),
        ]
        early += [(d - 1, d, d, self.whole, d - 1) for d in range(1, n) if d not in (near, far, n - near)]
        late = [
            (n, near, near, self.low, near - 1),
            (n + 1, n - near, n - near, self.high, n - near - 1),
        ]
        return early, late

    def nearest_first(self):
        return sorted(range(1, self.n), key=lambda d: -min(d, self.n - d))

    def give(self, copy):
        number, d, owner, (first, count), slot = copy
        start = self.run(self.member(owner)) + first
        return self.remote(
            self.held[f"sum{self.k}"].at[pl.ds(start, count)],
            self.held[f"in{self.k}"].at[slot, pl.ds(first, count)],
            "rs", number, d,
        )

    def reduce_start(self):
        for copy in self.given()[0]:
            self.among(self.member(copy[2]), lambda: self.give(copy).start())

    def reduce_relay(self):
        early, late = self.given()
        for passed, copy in zip(early, late):
            self.give(passed).wait_recv()
            _, _, owner, (first, count), _ = copy
            tiles = pl.ds(self.run(self.member(owner)) + first, count)
            came = self.held[f"in{self.k}"][self.far - 1, pl.ds(first, count)]
            held = self.held[f"sum{self.k}"]
            held[tiles] = (held[tiles].astype(jnp.float32) + came.astype(jnp.float32)).astype(jnp.bfloat16)
            self.give(copy).start()

    def reduce_finish(self):
        k, early, late = self.k, *self.given()

        def receive():
            for copy in early[len(late):] + late:
                self.give(copy).wait_recv()
            total = self.held[f"sum{k}"][pl.ds(self.run(self.me), self.take)].astype(jnp.float32)
            for d in range(1, self.n):
                if not (self.relay and d == self.far):
                    total += self.held[f"in{k}"][d - 1].astype(jnp.float32)
            total = total.astype(jnp.bfloat16)
            if k < 2:
                self.held[f"sum{k + 1}"][...] = total
            else:
                self.held["all"][pl.ds(self.bases[3], self.take)] = total

        self.among(self.me, receive)

    def shown(self):
        if not self.relay:
            return [(d - 1, d, 0, self.whole) for d in self.nearest_first()], []
        n, far, near = self.n, self.far, self.far - 1
        early = [
            (near - 1, near, 0, self.low),
            (n - near - 1, n - near, 0, self.high),
            (n, near, 0, self.high),
            (n + 1, n - near, 0, self.low),
        ]
        early += [(d - 1, d, 0, self.whole) for d in range(1, n) if d not in (near, far, n - near)]
        late = [(far - 1, 1, near, self.low), (n - 1, n - 1, n - near, self.high)]
        return early, late

    def show(self, copy, arriving=False):
        number, d, back, (first, count) = copy
        source = self.member(2 * self.n - back - (d if arriving else 0))
        tiles = pl.ds(self.bases[self.k] + self.run(source) + first, count)
        return self.remote(self.held["all"].at[tiles], self.held["all"].at[tiles], "ag", number, d), source

    def gather_start(self):
        for copy in self.shown()[0]:
            self.among(self.me, lambda: self.show(copy)[0].start())

    def gather_relay(self):
        early, late = self.shown()
        for passed, copy in zip(early, late):
            self.show(passed, True)[0].wait_recv()
            self.show(copy)[0].start()

    def gather_finish(self):
        early, late = self.shown()
        for copy in early[len(late):] + late:
            source = self.member(2 * self.n - copy[2] - copy[1])
            self.among(source, lambda: self.show(copy, True)[0].wait_recv())

    def reduce_drain(self):
        for copy in sum(self.given(), []):
            self.among(self.member(copy[2]), lambda: self.give(copy).wait_send())

    def gather_drain(self):
        for copy in sum(self.shown(), []):
            self.among(self.me, lambda: self.show(copy)[0].wait_send())


def steps_of(parts, scratch):
    steps = [[], [], []]
    for part, held in zip(parts, scratch):
        i1, i2, i3 = (lax.axis_index(axis) for axis in part.order)
        t1, t2, t3 = part.take
        bases = (0, i1 * t1, i1 * t1 + i2 * t2, i1 * t1 + i2 * t2 + i3 * t3)
        for k in range(3):
            steps[k].append(Step(part, held, k, bases))
    return steps


def sum_over_chips(steps, meanwhile):
    for step in steps[0]:
        if step.relay:
            step.reduce_relay()
    write_out = meanwhile()
    for k in range(3):
        for i, step in enumerate(steps[k]):
            step.reduce_finish()
            if k < 2:
                steps[k + 1][i].reduce_start()
            else:
                step.gather_start()
        for step in steps[k]:
            step.reduce_drain()
        if k == 0:
            end = write_out()
    for k in (2, 1, 0):
        for i, step in enumerate(steps[k]):
            if step.relay:
                step.gather_relay()
        for i, step in enumerate(steps[k]):
            step.gather_finish()
            if k > 0:
                steps[k - 1][i].gather_start()
        if k == 1:
            end()
        if k > 0:
            for step in steps[k]:
                step.gather_drain()
    for step in steps[0]:
        step.gather_drain()


def exchange(
    parts, sizes,
    queries, key_in, values, ids_in, grad_out, weight, patches,
    returned, *rest,
):
    core = lax.axis_index("fsdp")
    other = 1 - core
    half = weight.shape[0]
    length = queries.shape[0]
    near, scratch = rest[len(parts):]
    scratch = [{**held, "all": total} for held, total in zip(scratch, rest)]
    steps = steps_of(parts, scratch)
    sems = near["sems"]

    barrier = pltpu.get_barrier_semaphore()
    greeted = 0
    for axis, n in sizes.items():
        me = lax.axis_index(axis)
        for d in range(1, n):
            pl.semaphore_signal(
                barrier, inc=1, device_id={axis: lax.rem(me + d, n)}, device_id_type=MESH
            )
            greeted += 1

    def local(source, target, number):
        copy = pltpu.make_async_copy(source, target, sems.at[number])
        copy.start()
        return copy

    ids_here = local(ids_in, near["ids"], 12)
    arrays_here = [
        local(array, near["arrays"].at[i], 13 + i) for i, array in enumerate((queries, key_in, values))
    ]
    grad_out_here = local(grad_out, near["grad_out"].at[0], 0)
    weight_here = local(weight, near["weight"].at[0], 1)
    patches_here = local(patches, near["patches"], 2)

    ids_here.wait()
    ids = jnp.broadcast_to(near["ids"][0:1].astype(jnp.float32), (length, length))
    near["hidden"][...] = jnp.where(ids == ids.T, 0.0, -1e30)
    for copy in arrays_here:
        copy.wait()
    arrays = *(near["arrays"].at[i] for i in range(3)), near["hidden"]
    attend_heads(*arrays, near["attended"].at[1], other * half)

    pl.semaphore_wait(barrier, greeted)

    def across(source, target, number):
        copy = pltpu.make_async_remote_copy(
            src_ref=source,
            dst_ref=target,
            send_sem=sems.at[number],
            recv_sem=sems.at[number + 1],
            device_id={"fsdp": other},
            device_id_type=MESH,
        )
        copy.start()
        return copy

    attended_there = across(near["attended"].at[1], near["attended"].at[2], 3)
    grad_out_there = across(grad_out, near["grad_out"].at[1], 5)
    weight_there = across(weight, near["weight"].at[1], 7)
    attend_heads(*arrays, near["attended"].at[0], core * half)

    grad_out_here.wait()
    attended_there.wait_recv()
    grad_out_there.wait_recv()
    rows_in = (((0,), (0,)), ((), ()))
    for part, held, step in zip(parts, scratch, steps[0]):
        columns = pl.ds(part.first * LANE, part.blocks * LANE)
        product = lax.dot_general(
            near["attended"][0], near["grad_out"][0, :, columns], rows_in,
            preferred_element_type=jnp.float32,
        ) + lax.dot_general(
            near["attended"][2], near["grad_out"][1, :, columns], rows_in,
            preferred_element_type=jnp.float32,
        )
        product = product.astype(jnp.bfloat16)
        for block in range(part.blocks):
            held["sum0"][pl.ds(block * part.per_block, part.per_block)] = product[
                :, block * LANE:(block + 1) * LANE
            ].reshape(part.per_block, ROW, LANE)
        spare = part.padded - part.tiles
        if spare:
            held["sum0"][pl.ds(part.tiles, spare)] = jnp.zeros((spare, ROW, LANE), jnp.bfloat16)
        step.reduce_start()

    def encode():
        weight_here.wait()
        patches_here.wait()
        weight_there.wait_recv()
        projected = jnp.dot(
            near["attended"][0], near["weight"][0], preferred_element_type=jnp.float32
        ) + jnp.dot(near["attended"][1], near["weight"][1], preferred_element_type=jnp.float32)
        encoded = (near["patches"][...].astype(jnp.float32) + projected).astype(jnp.bfloat16)
        owner = near["ids"][1:2]
        earlier = (
            lax.broadcasted_iota(jnp.int32, (length, length), 0)
            < lax.broadcasted_iota(jnp.int32, (length, length), 1)
        ).astype(jnp.bfloat16)
        is_one = jnp.broadcast_to(owner, (ROW, length)).astype(jnp.float32).astype(jnp.bfloat16)
        ones_before = jnp.dot(is_one, earlier, preferred_element_type=jnp.float32)[:1]
        ones_before = ones_before.astype(jnp.int32)
        place = lax.broadcasted_iota(jnp.int32, (1, length), 1)
        rank = jnp.where(owner == 1, ones_before, place - ones_before)
        slot = lax.broadcasted_iota(jnp.int32, (length, length), 0)

        def placed(group):
            chosen = jnp.where(owner == group, rank, -1)
            onehot = (slot == chosen).astype(jnp.float32).astype(jnp.bfloat16)
            return jnp.dot(onehot, encoded, preferred_element_type=jnp.float32).astype(jnp.bfloat16)

        own_rows = pl.ds(pl.multiple_of(core * length, LANE), length)
        other_rows = pl.ds(pl.multiple_of(other * length, LANE), length)
        near["leaving"][...] = placed(other)
        rows_there = across(near["leaving"], near["returned"].at[own_rows], 9)
        near["returned"][own_rows] = placed(core)

        def write_out():
            rows_there.wait_recv()
            rows_out = local(near["returned"], returned, 11)

            def end():
                rows_there.wait_send()
                rows_out.wait()

            return end

        for copy in (attended_there, grad_out_there, weight_there):
            copy.wait_send()
        return write_out

    sum_over_chips(steps, encode)


def deliver(parts, factor, *refs):
    tiles, (rows, rows_out, gradient, held, rows_held, sems) = refs[:len(parts)], refs[len(parts):]
    rows_in = pltpu.make_async_copy(rows, rows_held, sems.at[0])
    rows_in.start()
    copies = []
    height = held.shape[1]
    deep = height // ROW
    for i in range(held.shape[0]):
        for part, total in zip(parts, tiles):
            for block in range(part.blocks):
                held[i, :, pl.ds((part.first + block) * LANE, LANE)] = (
                    total[pl.ds(block * part.per_block + i * deep, deep)]
                    .reshape(height, LANE).astype(jnp.float32) * factor
                )
        copy = pltpu.make_async_copy(held.at[i], gradient.at[pl.ds(i * height, height)], sems.at[i + 1])
        copy.start()
        copies.append(copy)
        if i == 0:
            rows_in.wait()
            rows_copy = pltpu.make_async_copy(rows_held, rows_out, sems.at[held.shape[0] + 1])
            rows_copy.start()
            copies.append(rows_copy)
    for copy in copies:
        copy.wait()


def per_device(patches, queries, key_in, values, windows, out_weight, owners, grad_out):
    sizes = {axis: lax.axis_size(axis) for axis in ("fsdp", "x", "y", "z")}
    length, width = patches.shape
    half = out_weight.shape[0]
    parts, first = [], 0
    for blocks, order in PARTS:
        parts.append(Part(first, blocks, order, sizes, half))
        first += blocks
    factor = 1.0 / math.sqrt(length * math.prod(sizes.values()))
    bf16 = jnp.bfloat16
    near = {
        "weight": pltpu.VMEM((2, half, width), bf16),
        "patches": pltpu.VMEM((length, width), bf16),
        "ids": pltpu.VMEM((2, length), jnp.int32),
        "arrays": pltpu.VMEM((3, length, width), bf16),
        "hidden": pltpu.VMEM((length, length), jnp.float32),
        "attended": pltpu.VMEM((3, length, half), bf16),
        "grad_out": pltpu.VMEM((2, length, width), bf16),
        "leaving": pltpu.VMEM((length, width), bf16),
        "returned": pltpu.VMEM((2 * length, width), bf16),
        "sems": pltpu.SemaphoreType.DMA((16,)),
    }
    vmem, anywhere, hbm = (
        pl.BlockSpec(memory_space=space) for space in (pltpu.VMEM, pl.ANY, pltpu.HBM)
    )
    params = dict(has_side_effects=True, vmem_limit_bytes=52 * 1024 * 1024)
    returned, *tiles = pl.pallas_call(
        functools.partial(exchange, parts, sizes),
        out_shape=(
            jax.ShapeDtypeStruct((2 * length, width), bf16),
            *(jax.ShapeDtypeStruct((part.padded, ROW, LANE), bf16) for part in parts),
        ),
        in_specs=[hbm] * 7,
        out_specs=(anywhere, *[vmem] * len(parts)),
        scratch_shapes=[near, [part.scratch() for part in parts]],
        compiler_params=pltpu.CompilerParams(collective_id=0, **params),
        name="exchange",
    )(queries, key_in, values, jnp.stack([windows[0], owners[:, 0]]), grad_out, out_weight, patches)
    chunks = 4
    return pl.pallas_call(
        functools.partial(deliver, parts, factor),
        out_shape=(
            jax.ShapeDtypeStruct((2 * length, width), bf16),
            jax.ShapeDtypeStruct((half, width), jnp.float32),
        ),
        in_specs=[*[vmem] * len(parts), anywhere],
        out_specs=(anywhere, anywhere),
        scratch_shapes=[
            pltpu.VMEM((chunks, half // chunks, width), jnp.float32),
            pltpu.VMEM((2 * length, width), bf16),
            pltpu.SemaphoreType.DMA((chunks + 2,)),
        ],
        compiler_params=pltpu.CompilerParams(**params),
        name="deliver",
    )(*tiles, returned)


def solution(mesh):
    chips = mesh.devices.reshape(12, 8, 4, 2)
    grid = Mesh(chips, ("z", "y", "x", "fsdp"))
    rows = P(("z", "y", "x", "fsdp"), None)
    return jax.shard_map(
        per_device,
        mesh=grid,
        in_specs=(rows, rows, rows, rows, rows, P("fsdp", None), rows, rows),
        out_specs=(rows, P("fsdp", None)),
        check_vma=False,
    )
```

```python
import functools
import math

import jax
import jax.numpy as jnp
from jax import lax
from jax.experimental import pallas as pl
from jax.experimental.pallas import tpu as pltpu
from jax.sharding import Mesh
from jax.sharding import PartitionSpec as P

HEADS = 16
HEAD_DIM = 80
MESH = pl.DeviceIdType.MESH
ROW, LANE = 16, 128
PARTS = ((4, ("x", "y", "z")), (2, ("y", "x", "z")), (4, ("x", "y", "z")))


def attend_heads(queries, key_in, values, hidden, attended, base):
    width = attended.shape[1]
    pending = {}
    for head in range(width // HEAD_DIM):
        begin = head * HEAD_DIM
        first, last = begin // LANE, (begin + HEAD_DIM - 1) // LANE
        span = (last - first + 1) * LANE
        columns = pl.ds(pl.multiple_of(base + first * LANE, LANE), span)
        place = lax.broadcasted_iota(jnp.int32, (1, span), 1) + (first * LANE - begin)
        own = ((place >= 0) & (place < HEAD_DIM)).astype(jnp.float32).astype(jnp.bfloat16)
        scores = lax.dot_general(
            queries[:, columns] * own, key_in[:, columns], (((1,), (1,)), ((), ())),
            preferred_element_type=jnp.float32,
        ) * (1.0 / math.sqrt(HEAD_DIM)) + hidden[...]
        expo = jnp.exp(scores - jnp.max(scores, axis=1, keepdims=True))
        weights = (expo * (1.0 / jnp.sum(expo, axis=1, keepdims=True))).astype(jnp.bfloat16)
        result = jnp.dot(weights, values[:, columns] * own, preferred_element_type=jnp.float32)
        for block in range(first, last + 1):
            piece = result[:, (block - first) * LANE:(block - first + 1) * LANE]
            pending[block] = pending[block] + piece if block in pending else piece
            if (block + 1) * LANE <= begin + HEAD_DIM:
                attended[:, block * LANE:(block + 1) * LANE] = pending.pop(block).astype(jnp.bfloat16)


class Part:
    def __init__(self, first, blocks, order, sizes, rows):
        self.first, self.blocks, self.order = first, blocks, order
        self.per_block = rows // ROW
        self.tiles = blocks * self.per_block
        n = [sizes[axis] for axis in order]
        self.n = n
        t3 = -(-self.tiles // math.prod(n))
        t2 = -(-self.tiles // (n[0] * n[1]))
        t2 = -(-t2 // t3) * t3
        t1 = n[1] * t2
        self.take = (t1, t2, t3)
        self.owners = (n[0], n[1], t2 // t3)
        self.padded = n[0] * t1
        self.relay = tuple(
            k == 0 and n[k] % 2 == 0 and n[k] >= 4 and self.take[k] >= 2
            for k in range(3)
        )

    def scratch(self):
        held = {"sum0": pltpu.VMEM((self.padded, ROW, LANE), jnp.bfloat16)}
        for k in range(3):
            n, take = self.n[k], self.take[k]
            held[f"in{k}"] = pltpu.VMEM((n - 1, take, ROW, LANE), jnp.bfloat16)
            if k < 2:
                held[f"sum{k + 1}"] = pltpu.VMEM((take, ROW, LANE), jnp.bfloat16)
            for name in ("rs_send", "rs_recv", "ag_send", "ag_recv"):
                held[f"{name}{k}"] = pltpu.SemaphoreType.DMA((n + 2,))
        return held


class Step:
    def __init__(self, part, held, k, bases):
        self.part, self.held, self.k, self.bases = part, held, k, bases
        self.axis, self.n, self.take, self.owners = part.order[k], part.n[k], part.take[k], part.owners[k]
        self.relay, self.everyone = part.relay[k], part.owners[k] == part.n[k]
        self.me = lax.axis_index(self.axis)
        self.far = self.n // 2
        half = self.take // 2
        self.low, self.high = (0, half), (half, self.take - half)
        self.whole = (0, self.take)

    def member(self, d):
        return lax.rem(self.me + d, self.n)

    def run(self, member):
        return (member if self.everyone else jnp.minimum(member, self.owners - 1)) * self.take

    def among(self, member, step):
        if self.everyone:
            step()
        else:
            pl.when(member < self.owners)(step)

    def remote(self, source, target, kind, number, d):
        return pltpu.make_async_remote_copy(
            src_ref=source,
            dst_ref=target,
            send_sem=self.held[f"{kind}_send{self.k}"].at[number],
            recv_sem=self.held[f"{kind}_recv{self.k}"].at[number],
            device_id={self.axis: self.member(d)},
            device_id_type=MESH,
        )

    def given(self):
        if not self.relay:
            return [(d - 1, d, d, self.whole, d - 1) for d in self.nearest_first()], []
        n, far, near = self.n, self.far, self.far - 1
        early = [
            (far - 1, 1, far, self.low, far - 1),
            (n - 1, n - 1, far, self.high, far - 1),
            (near - 1, near, near, self.high, near - 1),
            (n - near - 1, n - near, n - near, self.low, n - near - 1),
        ]
        early += [(d - 1, d, d, self.whole, d - 1) for d in range(1, n) if d not in (near, far, n - near)]
        late = [
            (n, near, near, self.low, near - 1),
            (n + 1, n - near, n - near, self.high, n - near - 1),
        ]
        return early, late

    def nearest_first(self):
        return sorted(range(1, self.n), key=lambda d: -min(d, self.n - d))

    def give(self, copy):
        number, d, owner, (first, count), slot = copy
        start = self.run(self.member(owner)) + first
        return self.remote(
            self.held[f"sum{self.k}"].at[pl.ds(start, count)],
            self.held[f"in{self.k}"].at[slot, pl.ds(first, count)],
            "rs", number, d,
        )

    def reduce_start(self):
        for copy in self.given()[0]:
            self.among(self.member(copy[2]), lambda: self.give(copy).start())

    def reduce_relay(self):
        early, late = self.given()
        for passed, copy in zip(early, late):
            self.give(passed).wait_recv()
            _, _, owner, (first, count), _ = copy
            tiles = pl.ds(self.run(self.member(owner)) + first, count)
            came = self.held[f"in{self.k}"][self.far - 1, pl.ds(first, count)]
            held = self.held[f"sum{self.k}"]
            held[tiles] = (held[tiles].astype(jnp.float32) + came.astype(jnp.float32)).astype(jnp.bfloat16)
            self.give(copy).start()

    def reduce_finish(self):
        k, early, late = self.k, *self.given()

        def receive():
            for copy in early[len(late):] + late:
                self.give(copy).wait_recv()
            total = self.held[f"sum{k}"][pl.ds(self.run(self.me), self.take)].astype(jnp.float32)
            for d in range(1, self.n):
                if not (self.relay and d == self.far):
                    total += self.held[f"in{k}"][d - 1].astype(jnp.float32)
            total = total.astype(jnp.bfloat16)
            if k < 2:
                self.held[f"sum{k + 1}"][...] = total
            else:
                self.held["all"][pl.ds(self.bases[3], self.take)] = total

        self.among(self.me, receive)

    def shown(self):
        if not self.relay:
            return [(d - 1, d, 0, self.whole) for d in self.nearest_first()], []
        n, far, near = self.n, self.far, self.far - 1
        early = [
            (near - 1, near, 0, self.low),
            (n - near - 1, n - near, 0, self.high),
            (n, near, 0, self.high),
            (n + 1, n - near, 0, self.low),
        ]
        early += [(d - 1, d, 0, self.whole) for d in range(1, n) if d not in (near, far, n - near)]
        late = [(far - 1, 1, near, self.low), (n - 1, n - 1, n - near, self.high)]
        return early, late

    def show(self, copy, arriving=False):
        number, d, back, (first, count) = copy
        source = self.member(2 * self.n - back - (d if arriving else 0))
        tiles = pl.ds(self.bases[self.k] + self.run(source) + first, count)
        return self.remote(self.held["all"].at[tiles], self.held["all"].at[tiles], "ag", number, d), source

    def gather_start(self):
        for copy in self.shown()[0]:
            self.among(self.me, lambda: self.show(copy)[0].start())

    def gather_relay(self):
        early, late = self.shown()
        for passed, copy in zip(early, late):
            self.show(passed, True)[0].wait_recv()
            self.show(copy)[0].start()

    def gather_finish(self):
        early, late = self.shown()
        for copy in early[len(late):] + late:
            source = self.member(2 * self.n - copy[2] - copy[1])
            self.among(source, lambda: self.show(copy, True)[0].wait_recv())

    def reduce_drain(self):
        for copy in sum(self.given(), []):
            self.among(self.member(copy[2]), lambda: self.give(copy).wait_send())

    def gather_drain(self):
        for copy in sum(self.shown(), []):
            self.among(self.me, lambda: self.show(copy)[0].wait_send())


def steps_of(parts, scratch):
    steps = [[], [], []]
    for part, held in zip(parts, scratch):
        i1, i2, i3 = (lax.axis_index(axis) for axis in part.order)
        t1, t2, t3 = part.take
        bases = (0, i1 * t1, i1 * t1 + i2 * t2, i1 * t1 + i2 * t2 + i3 * t3)
        for k in range(3):
            steps[k].append(Step(part, held, k, bases))
    return steps


def sum_over_chips(steps, meanwhile):
    for step in steps[0]:
        if step.relay:
            step.reduce_relay()
    write_out = meanwhile()
    for k in range(3):
        for i, step in enumerate(steps[k]):
            step.reduce_finish()
            if k < 2:
                steps[k + 1][i].reduce_start()
            else:
                step.gather_start()
        for step in steps[k]:
            step.reduce_drain()
        if k == 0:
            end = write_out()
    for k in (2, 1, 0):
        for i, step in enumerate(steps[k]):
            if step.relay:
                step.gather_relay()
        for i, step in enumerate(steps[k]):
            step.gather_finish()
            if k > 0:
                steps[k - 1][i].gather_start()
        if k == 1:
            end()
        if k > 0:
            for step in steps[k]:
                step.gather_drain()
    for step in steps[0]:
        step.gather_drain()


def exchange(
    parts, sizes,
    queries, key_in, values, ids_in, grad_out, weight, patches,
    returned, *rest,
):
    core = lax.axis_index("fsdp")
    other = 1 - core
    half = weight.shape[0]
    length = queries.shape[0]
    near, scratch = rest[len(parts):]
    scratch = [{**held, "all": total} for held, total in zip(scratch, rest)]
    steps = steps_of(parts, scratch)
    sems = near["sems"]

    barrier = pltpu.get_barrier_semaphore()
    greeted = 0
    for axis, n in sizes.items():
        me = lax.axis_index(axis)
        for d in range(1, n):
            pl.semaphore_signal(
                barrier, inc=1, device_id={axis: lax.rem(me + d, n)}, device_id_type=MESH
            )
            greeted += 1

    def local(source, target, number):
        copy = pltpu.make_async_copy(source, target, sems.at[number])
        copy.start()
        return copy

    ids_here = local(ids_in, near["ids"], 12)
    arrays_here = [
        local(array, near["arrays"].at[i], 13 + i) for i, array in enumerate((queries, key_in, values))
    ]
    grad_out_here = local(grad_out, near["grad_out"].at[0], 0)
    weight_here = local(weight, near["weight"].at[0], 1)
    patches_here = local(patches, near["patches"], 2)

    ids_here.wait()
    ids = jnp.broadcast_to(near["ids"][0:1].astype(jnp.float32), (length, length))
    near["hidden"][...] = jnp.where(ids == ids.T, 0.0, -1e30)
    for copy in arrays_here:
        copy.wait()
    arrays = *(near["arrays"].at[i] for i in range(3)), near["hidden"]
    attend_heads(*arrays, near["attended"].at[1], other * half)
    near["turned"][1] = near["attended"][1].T

    pl.semaphore_wait(barrier, greeted)

    def across(source, target, number):
        copy = pltpu.make_async_remote_copy(
            src_ref=source,
            dst_ref=target,
            send_sem=sems.at[number],
            recv_sem=sems.at[number + 1],
            device_id={"fsdp": other},
            device_id_type=MESH,
        )
        copy.start()
        return copy

    attended_there = across(near["turned"].at[1], near["turned"].at[2], 3)
    grad_out_there = across(grad_out, near["grad_out"].at[1], 5)
    weight_there = across(weight, near["weight"].at[1], 7)
    attend_heads(*arrays, near["attended"].at[0], core * half)
    near["turned"][0] = near["attended"][0].T

    grad_out_here.wait()
    attended_there.wait_recv()
    grad_out_there.wait_recv()
    for part, held, step in zip(parts, scratch, steps[0]):
        columns = pl.ds(part.first * LANE, part.blocks * LANE)
        product = jnp.dot(
            near["turned"][0], near["grad_out"][0, :, columns], preferred_element_type=jnp.float32
        ) + jnp.dot(
            near["turned"][2], near["grad_out"][1, :, columns], preferred_element_type=jnp.float32
        )
        product = product.astype(jnp.bfloat16)
        for block in range(part.blocks):
            held["sum0"][pl.ds(block * part.per_block, part.per_block)] = product[
                :, block * LANE:(block + 1) * LANE
            ].reshape(part.per_block, ROW, LANE)
        spare = part.padded - part.tiles
        if spare:
            held["sum0"][pl.ds(part.tiles, spare)] = jnp.zeros((spare, ROW, LANE), jnp.bfloat16)
        step.reduce_start()

    def encode():
        weight_here.wait()
        patches_here.wait()
        weight_there.wait_recv()
        projected = jnp.dot(
            near["attended"][0], near["weight"][0], preferred_element_type=jnp.float32
        ) + jnp.dot(near["attended"][1], near["weight"][1], preferred_element_type=jnp.float32)
        encoded = (near["patches"][...].astype(jnp.float32) + projected).astype(jnp.bfloat16)
        owner = near["ids"][1:2]
        earlier = (
            lax.broadcasted_iota(jnp.int32, (length, length), 0)
            < lax.broadcasted_iota(jnp.int32, (length, length), 1)
        ).astype(jnp.bfloat16)
        is_one = jnp.broadcast_to(owner, (ROW, length)).astype(jnp.float32).astype(jnp.bfloat16)
        ones_before = jnp.dot(is_one, earlier, preferred_element_type=jnp.float32)[:1]
        ones_before = ones_before.astype(jnp.int32)
        place = lax.broadcasted_iota(jnp.int32, (1, length), 1)
        rank = jnp.where(owner == 1, ones_before, place - ones_before)
        slot = lax.broadcasted_iota(jnp.int32, (length, length), 0)

        def placed(group):
            chosen = jnp.where(owner == group, rank, -1)
            onehot = (slot == chosen).astype(jnp.float32).astype(jnp.bfloat16)
            return jnp.dot(onehot, encoded, preferred_element_type=jnp.float32).astype(jnp.bfloat16)

        own_rows = pl.ds(pl.multiple_of(core * length, LANE), length)
        other_rows = pl.ds(pl.multiple_of(other * length, LANE), length)
        near["leaving"][...] = placed(other)
        rows_there = across(near["leaving"], near["returned"].at[own_rows], 9)
        near["returned"][own_rows] = placed(core)

        def write_out():
            rows_there.wait_recv()
            rows_out = local(near["returned"], returned, 11)

            def end():
                rows_there.wait_send()
                rows_out.wait()

            return end

        for copy in (attended_there, grad_out_there, weight_there):
            copy.wait_send()
        return write_out

    sum_over_chips(steps, encode)


def deliver(parts, factor, *refs):
    tiles, (gradient, held, sems) = refs[:len(parts)], refs[len(parts):]
    copies = []
    height = held.shape[1]
    deep = height // ROW
    for i in range(held.shape[0]):
        for part, total in zip(parts, tiles):
            for block in range(part.blocks):
                held[i, :, pl.ds((part.first + block) * LANE, LANE)] = (
                    total[pl.ds(block * part.per_block + i * deep, deep)]
                    .reshape(height, LANE).astype(jnp.float32) * factor
                )
        copy = pltpu.make_async_copy(held.at[i], gradient.at[pl.ds(i * height, height)], sems.at[i])
        copy.start()
        copies.append(copy)
    for copy in copies:
        copy.wait()


def per_device(patches, queries, key_in, values, windows, out_weight, owners, grad_out):
    sizes = {axis: lax.axis_size(axis) for axis in ("fsdp", "x", "y", "z")}
    length, width = patches.shape
    half = out_weight.shape[0]
    parts, first = [], 0
    for blocks, order in PARTS:
        parts.append(Part(first, blocks, order, sizes, half))
        first += blocks
    factor = 1.0 / math.sqrt(length * math.prod(sizes.values()))
    bf16 = jnp.bfloat16
    near = {
        "weight": pltpu.VMEM((2, half, width), bf16),
        "patches": pltpu.VMEM((length, width), bf16),
        "ids": pltpu.VMEM((2, length), jnp.int32),
        "arrays": pltpu.VMEM((3, length, width), bf16),
        "hidden": pltpu.VMEM((length, length), jnp.float32),
        "attended": pltpu.VMEM((2, length, half), bf16),
        "turned": pltpu.VMEM((3, half, length), bf16),
        "grad_out": pltpu.VMEM((2, length, width), bf16),
        "leaving": pltpu.VMEM((length, width), bf16),
        "returned": pltpu.VMEM((2 * length, width), bf16),
        "sems": pltpu.SemaphoreType.DMA((16,)),
    }
    vmem, anywhere, hbm = (
        pl.BlockSpec(memory_space=space) for space in (pltpu.VMEM, pl.ANY, pltpu.HBM)
    )
    params = dict(has_side_effects=True, vmem_limit_bytes=52 * 1024 * 1024)
    returned, *tiles = pl.pallas_call(
        functools.partial(exchange, parts, sizes),
        out_shape=(
            jax.ShapeDtypeStruct((2 * length, width), bf16),
            *(jax.ShapeDtypeStruct((part.padded, ROW, LANE), bf16) for part in parts),
        ),
        in_specs=[hbm] * 7,
        out_specs=(anywhere, *[vmem] * len(parts)),
        scratch_shapes=[near, [part.scratch() for part in parts]],
        compiler_params=pltpu.CompilerParams(collective_id=0, **params),
        name="exchange",
    )(queries, key_in, values, jnp.stack([windows[0], owners[:, 0]]), grad_out, out_weight, patches)
    chunks = 4
    gradient = pl.pallas_call(
        functools.partial(deliver, parts, factor),
        out_shape=jax.ShapeDtypeStruct((half, width), jnp.float32),
        in_specs=[vmem] * len(parts),
        out_specs=anywhere,
        scratch_shapes=[
            pltpu.VMEM((chunks, half // chunks, width), jnp.float32),
            pltpu.SemaphoreType.DMA((chunks,)),
        ],
        compiler_params=pltpu.CompilerParams(**params),
        name="deliver",
    )(*tiles)
    return returned, gradient


def solution(mesh):
    chips = mesh.devices.reshape(12, 8, 4, 2)
    grid = Mesh(chips, ("z", "y", "x", "fsdp"))
    rows = P(("z", "y", "x", "fsdp"), None)
    return jax.shard_map(
        per_device,
        mesh=grid,
        in_specs=(rows, rows, rows, rows, rows, P("fsdp", None), rows, rows),
        out_specs=(rows, P("fsdp", None)),
        check_vma=False,
    )
```
